32 devices in a mesh: groups: 2 (over x), gx: 4 (over y, core), gy: 4 (over z).
Axes of the slice: x: 2, y: 2, z: 4, core: 2. Of those that a mesh axis runs over, the one named last changes fastest.
Arguments:
- probes: bfloat16 [128, 16, 3, 512], P(('groups', 'gx', 'gy')), parts along dimension 0, may hold values from -6 to 6
- positions: float32 [128, 3, 512], P(('groups', 'gx', 'gy')), parts along dimension 0, may hold values from -4 to 130, as said below
- polar: float32 [128, 512], P(('groups', 'gx', 'gy')), parts along dimension 0, may hold values from 0.5 to 8
- basis: bfloat16 [128, 64, 3, 512], P(('groups', 'gx', 'gy')), parts along dimension 0, may hold values from -0.25 to 0.25
- leaf_transfer: bfloat16 [128, 64, 64], P(('groups', 'gx', 'gy')), parts along dimension 0, may hold values from -0.375 to 0.375
- cluster_transfer: bfloat16 [32, 64, 64], P(('groups', 'gx', 'gy')), parts along dimension 0, may hold values from -0.5 to 0.5
- upper_transfer: bfloat16 [24, 64, 64], P('groups'), parts along dimension 0, may hold values from -0.5 to 0.5
- cluster_coupling: bfloat16 [32, 6, 64, 64], P(('groups', 'gx', 'gy')), parts along dimension 0, may hold values from -0.3125 to 0.3125
- upper_coupling: bfloat16 [28, 6, 64, 64], P('groups'), parts along dimension 0, may hold values from -0.3125 to 0.3125
- near_lists: int32 [128, 6], P(('groups', 'gx', 'gy')), parts along dimension 0, may hold values from -1 to 63, as said below
- cluster_lists: int32 [32, 6], P(('groups', 'gx', 'gy')), parts along dimension 0, may hold values from 0 to 15, as said below
- upper_lists: int32 [28, 6], P('groups'), parts along dimension 0, may hold values from 0 to 7, as said below
Outputs:
- applied: bfloat16 [128, 16, 3, 512], P(('groups', 'gx', 'gy')), parts along dimension 0
The draws below stay inside these ranges and needn't reach their ends.
There are 2 independent parts, one for each index of `groups`. The reference program is written for one: setup_inputs(seed, part) draws one part's arguments, and reference() takes and returns one part's arrays. A program takes and returns all parts, laid end to end along the dimension named above; each array names one. Nothing has to cross between parts.
Inputs may be any that keep to these rules, and one draw needn't show every extreme that they name: `near_lists`: slot 0 of row t names t itself; the following slots name leaves within 4 of t; after the named slots (at least 2) the row holds -1; all leaves of one device name equally many, some device names all 6 and some only 2. `cluster_lists`: row n names clusters within 4 of n, slot 0 names n itself. `upper_lists`: rows of level l (l = 1 to 3, 16 >> l rows each) follow those of lower levels; the row of node n names nodes of the same level within 4 of n, slot 0 names n itself. `positions`: atoms of leaf t have first coordinate within 4 of 2 t and the others within 4 of 0.
All inputs are finite; a program needn't handle non-finite values.
Results may differ from the reference program's by a relative error of at most 0.0057.
Values may be sent and summed in bfloat16 or wider, within the bound.
A program may use at most 128 MiB of HBM per device.

```python
import math
import jax
import jax.numpy as jnp
from jax import lax

LEAF = 512
RANK = 64
NV = 16
LEAF_DEV = 4
NEAR = 6
FAR = 6
REACH = 4
CREACH = 4
UP = 3
NODES = 16
LEAVES = 64
UPN = 14
UTN = 12


def far_rows(key, count):
    offsets = jax.random.randint(key, (count, FAR), -CREACH, CREACH + 1)
    offsets = offsets.at[:, 0].set(0)
    nodes = jnp.arange(count, dtype=jnp.int32)[:, None]
    return jnp.clip(nodes + offsets, 0, count - 1).astype(jnp.int32)


def draw_positions(key, part):
    key = jax.random.fold_in(key, 5)
    centre = 2.0 * jnp.arange(LEAVES, dtype=jnp.float32)
    spread = jax.random.uniform(key, (LEAVES, 3, LEAF), jnp.float32, -4.0, 4.0)
    offset_part = jnp.zeros((LEAVES, 3, 1), jnp.float32).at[:, 0, 0].set(centre)
    return spread + offset_part


def draw_near_lists(key, part):
    key = jax.random.fold_in(key, 7)
    key_class, key_order = jax.random.split(key)
    classes = jax.random.randint(key_class, (NODES,), 0, 3)
    classes = classes.at[0].set(2).at[NODES - 1].set(0)
    counts = jnp.repeat(2 + (NEAR - 2) * classes // 2, LEAF_DEV)
    keys = jax.random.split(key_order, LEAVES)
    orders = jax.vmap(lambda single: jax.random.permutation(single, 2 * REACH))(keys)
    offsets = orders - REACH
    offsets = offsets + (offsets >= 0).astype(offsets.dtype)
    leaf_ids = jnp.arange(LEAVES, dtype=jnp.int32)[:, None]
    picked = jnp.clip(leaf_ids + offsets[:, :NEAR - 1], 0, LEAVES - 1)
    full = jnp.concatenate([leaf_ids, picked], axis=1)
    slots = jnp.arange(NEAR, dtype=jnp.int32)[None, :]
    return jnp.where(slots < counts[:, None], full, -1).astype(jnp.int32)


def draw_cluster_lists(key, part):
    key = jax.random.fold_in(key, 9)
    return far_rows(key, NODES)


def draw_upper_lists(key, part):
    key = jax.random.fold_in(key, 13)
    blocks = []
    for level_index in range(1, UP + 1):
        blocks.append(far_rows(jax.random.fold_in(key, level_index), NODES >> level_index))
    return jnp.concatenate(blocks, axis=0)


def level_of(rng, shape, shards, least, largest):
    gain, own = 1.0, jax.random.fold_in(rng, 6)
    for position, parts in shards:
        steps = jnp.exp(jax.random.uniform(jax.random.fold_in(own, position), (parts,), jnp.float32, least / len(shards), largest / len(shards)))
        gain = gain * jnp.repeat(steps, shape[position] // parts).reshape([-1 if axis == position else 1 for axis in range(len(shape))])
    return gain


def scatter_about(rng, dims, scale, most, cuts=(), held_as=jnp.bfloat16):
    gain = level_of(rng, dims, cuts, -0.22, 0.18) if cuts else 1.0
    values = jax.random.normal(rng, dims, jnp.float32) * scale * gain
    return jnp.minimum(jnp.maximum(values, -most), most).astype(held_as)


def setup_inputs(seed: int = 0, part: int = 0) -> dict:
    streams_of = jax.random.split(jax.random.key(seed), 13)
    part_splits = jax.random.split(jax.random.fold_in(streams_of[12], part), 13)
    probes = scatter_about(part_splits[0], (LEAVES, NV, 3, LEAF), 1.0, 6.0, ((0, 16),))
    positions = draw_positions(jax.random.fold_in(jax.random.fold_in(streams_of[12], part), 71), part)
    polar = jnp.clip(jnp.exp(math.log(8.0) - 2.7725887 * jax.random.uniform(part_splits[2], (LEAVES, LEAF), jnp.float32) ** level_of(part_splits[2], (LEAVES, LEAF), ((0, 16),), -0.2, 0.2)), 0.5, 8.0)
    basis = scatter_about(part_splits[3], (LEAVES, RANK, 3, LEAF), LEAF ** -0.5, 0.25, ((0, 16),))
    leaf_transfer = scatter_about(part_splits[4], (LEAVES, RANK, RANK), (4 * RANK) ** -0.5, 0.375, ((0, 16),))
    cluster_transfer = scatter_about(part_splits[5], (NODES, RANK, RANK), (2 * RANK) ** -0.5, 0.5, ((0, 16),))
    upper_transfer = scatter_about(part_splits[6], (UTN, RANK, RANK), (2 * RANK) ** -0.5, 0.5)
    cluster_coupling = scatter_about(part_splits[7], (NODES, FAR, RANK, RANK), (FAR * RANK) ** -0.5, 0.3125, ((0, 16),))
    upper_coupling = scatter_about(part_splits[8], (UPN, FAR, RANK, RANK), (FAR * RANK) ** -0.5, 0.3125)
    near_lists = draw_near_lists(jax.random.fold_in(jax.random.fold_in(streams_of[12], part), 71), part)
    cluster_lists = draw_cluster_lists(jax.random.fold_in(jax.random.fold_in(streams_of[12], part), 71), part)
    upper_lists = draw_upper_lists(jax.random.fold_in(jax.random.fold_in(streams_of[12], part), 71), part)
    return {"probes": probes, "positions": positions, "polar": polar, "basis": basis, "leaf_transfer": leaf_transfer, "cluster_transfer": cluster_transfer, "upper_transfer": upper_transfer, "cluster_coupling": cluster_coupling, "upper_coupling": upper_coupling, "near_lists": near_lists, "cluster_lists": cluster_lists, "upper_lists": upper_lists}


SOFTEN = 1.0
HIGH = lax.Precision.HIGHEST

def dipole_block(target_pos, source_pos):
    leaf_size = target_pos.shape[1]
    between = target_pos[:, :, None] - source_pos[:, None, :]
    radius = lax.optimization_barrier(jnp.sum(between * between, axis=0)) + SOFTEN * SOFTEN
    weight = 1.0 / radius
    falloff = weight * jnp.sqrt(weight)
    outer_part = 3.0 * between[:, :, None, :] * jnp.transpose(between, (1, 0, 2))[None, :, :, :] * (weight * falloff)[None, :, None, :]
    diagonal_part = jnp.eye(3, dtype=jnp.float32)[:, None, :, None] * falloff[None, :, None, :]
    return (outer_part - diagonal_part).reshape(3 * leaf_size, 3 * leaf_size).astype(jnp.bfloat16)

def near_field(flat, positions, near_lists):

    def one_leaf(index):

        def one_slot(total, source):
            living = source >= 0
            picked = jnp.maximum(source, 0)
            block = dipole_block(positions[index], positions[picked])
            term = jnp.dot(flat[picked], block.T, preferred_element_type=jnp.float32)
            return (total + jnp.where(living, term, jnp.zeros_like(term)), source)
        total, unused = lax.scan(one_slot, jnp.zeros(flat.shape[1:], jnp.float32), near_lists[index])
        return total
    return lax.map(one_leaf, jnp.arange(flat.shape[0], dtype=jnp.int32))

def couple(coefs_level, lists, coupling):
    sources = coefs_level[lists]
    return jnp.einsum('nsvl,nskl->nvk', sources, coupling.astype(jnp.float32), precision=HIGH)

def reference(probes, positions, polar, basis, leaf_transfer, cluster_transfer, upper_transfer, cluster_coupling, upper_coupling, near_lists, cluster_lists, upper_lists):
    leaves = probes.shape[0]
    vectors = probes.shape[1]
    leaf_size = probes.shape[3]
    rank = basis.shape[1]
    root = jnp.sqrt(polar)
    scaled = (root[:, None, None, :] * probes.astype(jnp.float32)).astype(jnp.bfloat16)
    flat = scaled.reshape(leaves, vectors, 3 * leaf_size)
    basis_flat = basis.reshape(leaves, rank, 3 * leaf_size)
    near = near_field(flat, positions, near_lists)
    leaf_coef = jnp.einsum('tvc,tkc->tvk', flat.astype(jnp.float32), basis_flat.astype(jnp.float32), precision=HIGH)
    carried = jnp.einsum('tvl,tlk->tvk', leaf_coef, leaf_transfer.astype(jnp.float32), precision=HIGH)
    cluster = lax.optimization_barrier(jnp.sum(carried.reshape(NODES, LEAF_DEV, vectors, rank), axis=1))
    coefs = [cluster]
    lifted = jnp.einsum('nvl,nlk->nvk', cluster, cluster_transfer.astype(jnp.float32), precision=HIGH)
    transfers = [cluster_transfer]
    for level_index in range(1, UP + 1):
        current = lifted[0::2] + lifted[1::2]
        coefs.append(current)
        if level_index < UP:
            start = NODES - (NODES >> level_index - 1)
            count = NODES >> level_index
            upper_part = upper_transfer[start:start + count]
            transfers.append(upper_part)
            lifted = jnp.einsum('nvl,nlk->nvk', current, upper_part.astype(jnp.float32), precision=HIGH)
    fields = [couple(coefs[0], cluster_lists, cluster_coupling)]
    for level_index in range(1, UP + 1):
        start = NODES - (NODES >> level_index - 1)
        count = NODES >> level_index
        fields.append(couple(coefs[level_index], upper_lists[start:start + count], upper_coupling[start:start + count]))
    down = fields[UP]
    for level_index in range(UP - 1, -1, -1):
        spread = jnp.repeat(down, 2, axis=0)
        down = fields[level_index] + jnp.einsum('nvk,nlk->nvl', spread, transfers[level_index].astype(jnp.float32), precision=HIGH)
    leaf_field = jnp.einsum('tvk,tlk->tvl', jnp.repeat(down, LEAF_DEV, axis=0), leaf_transfer.astype(jnp.float32), precision=HIGH).astype(jnp.bfloat16)
    far = jnp.einsum('tvl,tlc->tvc', leaf_field.astype(jnp.float32), basis_flat.astype(jnp.float32), precision=HIGH)
    total = (near + far).reshape(leaves, vectors, 3, leaf_size)
    return (total * root[:, None, None, :]).astype(jnp.bfloat16)
```

```python
import functools

import jax
import jax.numpy as jnp
from jax import lax
from jax.experimental import pallas as pl
from jax.experimental.pallas import tpu as pltpu
from jax.sharding import PartitionSpec as P

UP = 3
FEATURES = 128
MESH = pl.DeviceIdType.MESH
F32 = jnp.float32
BF16 = jnp.bfloat16
VMEM = pl.BlockSpec(memory_space=pltpu.VMEM)
SMEM = pl.BlockSpec(memory_space=pltpu.SMEM)


def halves(value):
    high = value.astype(BF16)
    return high, (value - high.astype(F32)).astype(BF16)


def thirds(value):
    high, rest = value.astype(BF16).astype(F32), None
    rest = value - high
    middle = rest.astype(BF16).astype(F32)
    return high, middle, (rest - middle).astype(BF16).astype(F32)


def wide_dot(value, matrix, transposed):
    rows = value.shape[0]
    both = jnp.concatenate(halves(value), axis=0)
    dims = (((1,), (1 if transposed else 0,)), ((), ()))
    out = lax.dot_general(both, matrix, dims, preferred_element_type=F32)
    return out[:rows] + out[rows:]


def exchange(
    n,
    minor,
    probes,
    positions,
    polar,
    basis,
    leaf_transfer,
    cluster_transfer,
    wide,
    sites,
    coefs,
    coef_send,
    coef_recv,
    halo_send,
    halo_recv,
):
    leaves = probes.shape[0]
    me = lax.axis_index("gx") * minor + lax.axis_index("gy")

    def at(device):
        return {"gx": device // minor, "gy": lax.rem(device, minor)}

    barrier = pltpu.get_barrier_semaphore()

    @pl.loop(1, n)
    def _(k):
        pl.semaphore_signal(
            barrier, inc=1, device_id=at(lax.rem(me + k, n)), device_id_type=MESH
        )

    cluster = None
    for t in range(leaves):
        root = jnp.sqrt(polar[pl.ds(t, 1), :])
        coef = None
        for a in range(3):
            scaled = (root * probes[t, a].astype(F32)).astype(BF16)
            wide[leaves + t, a] = scaled
            part = lax.dot_general(
                scaled, basis[t, a], (((1,), (1,)), ((), ())), preferred_element_type=F32
            )
            coef = part if coef is None else coef + part
        carried = wide_dot(coef, leaf_transfer[t], False)
        cluster = carried if cluster is None else cluster + carried
    lifted = wide_dot(cluster, cluster_transfer[0], False)
    coefs[me] = jnp.concatenate([cluster, lifted], axis=1)
    sites[1] = jnp.zeros(sites.shape[1:], F32)
    for a in range(3):
        sites[1, pl.ds(a * leaves, leaves), :] = positions[a]
    pl.semaphore_wait(barrier, n - 1)

    def coef_copy(k, source):
        return pltpu.make_async_remote_copy(
            src_ref=coefs.at[source],
            dst_ref=coefs.at[source],
            send_sem=coef_send.at[k],
            recv_sem=coef_recv.at[source],
            device_id=at(lax.rem(me + k, n)),
            device_id_type=MESH,
        )

    def halo(side, device):
        return (
            pltpu.make_async_remote_copy(
                src_ref=wide.at[pl.ds(leaves, leaves)],
                dst_ref=wide.at[pl.ds(2 * leaves * side, leaves)],
                send_sem=halo_send.at[side, 0],
                recv_sem=halo_recv.at[side, 0],
                device_id=at(device),
                device_id_type=MESH,
            ),
            pltpu.make_async_remote_copy(
                src_ref=sites.at[1],
                dst_ref=sites.at[2 * side],
                send_sem=halo_send.at[side, 1],
                recv_sem=halo_recv.at[side, 1],
                device_id=at(device),
                device_id_type=MESH,
            ),
        )

    after = lax.rem(me + 1, n)
    before = lax.rem(me + n - 1, n)

    @pl.loop(1, n)
    def _(k):
        coef_copy(k, me).start()

    @pl.when(me < n - 1)
    def _():
        for copy in halo(0, after):
            copy.start()

    @pl.when(me > 0)
    def _():
        for copy in halo(1, before):
            copy.start()

    @pl.loop(1, n)
    def _(k):
        coef_copy(k, me).wait_send()
        coef_copy(k, lax.rem(me + k, n)).wait_recv()

    @pl.when(me < n - 1)
    def _():
        for copy in halo(0, after):
            copy.wait_send()
        for copy in halo(1, after):
            copy.wait_recv()

    @pl.when(me > 0)
    def _():
        for copy in halo(1, before):
            copy.wait_send()
        for copy in halo(0, before):
            copy.wait_recv()


def centred(sites, side, leaf, leaves, centre):
    point = [sites[side, pl.ds(a * leaves + leaf, 1), :] for a in range(3)]
    return [point[0] - centre] + point[1:]


def square(point):
    return point[0] * point[0] + point[1] * point[1] + point[2] * point[2]


def apply_operator(
    n,
    minor,
    near_lists,
    cluster_lists,
    upper_lists,
    wide,
    sites,
    coefs,
    polar,
    basis,
    leaf_transfer,
    cluster_transfer,
    upper_transfer,
    cluster_coupling,
    upper_coupling,
    out,
    moments,
    source_rows,
    target_rows,
    rows,
    total,
    level,
):
    leaves = polar.shape[0]
    slots = near_lists.shape[1]
    far_slots = cluster_lists.shape[1]
    vectors = wide.shape[2]
    leaf_size = wide.shape[3]
    rank = basis.shape[2]
    me = lax.axis_index("gx") * minor + lax.axis_index("gy")
    centre = (2 * leaves * me + leaves - 1).astype(F32)
    first = (me - 1) * leaves
    empty = 3 * leaves

    for node in range(n // 2):
        level[node] = coefs[2 * node, :, rank:] + coefs[2 * node + 1, :, rank:]
    for lev in range(1, UP):
        start = n - (n >> lev - 1)
        above = n - (n >> lev)
        for node in range(n >> lev + 1):
            place = start + 2 * node
            level[above + node] = wide_dot(
                level[place], upper_transfer[place], False
            ) + wide_dot(level[place + 1], upper_transfer[place + 1], False)
    fields = []
    for lev in range(UP + 1):
        start = n - (n >> lev - 1) if lev else 0
        place = start + (me >> lev)
        field = None
        for s in range(far_slots):
            if lev == 0:
                source = coefs[cluster_lists[0, s], :, :rank]
                matrix = cluster_coupling[0, s]
            else:
                source = level[start + upper_lists[s, place]]
                matrix = upper_coupling[place, s]
            term = wide_dot(source, matrix, True)
            field = term if field is None else field + term
        fields.append(field)
    down = fields[UP]
    for lev in range(UP - 1, -1, -1):
        if lev == 0:
            matrix = cluster_transfer[0]
        else:
            matrix = upper_transfer[n - (n >> lev - 1) + (me >> lev)]
        down = fields[lev] + wide_dot(down, matrix, True)

    rows[...] = jnp.zeros(rows.shape, F32)
    moments[empty] = jnp.zeros(moments.shape[1:], BF16)

    def fill(point, factor, own):
        base = 0
        for a in range(3):
            one, two, three = thirds(point[a] * factor)
            order = (one, one, two, two, one, three) if own else (one, two, one, two, three, one)
            for k, row in enumerate(order):
                rows[base + k : base + k + 1, :] = row
            base += 6
        norm = thirds(square(point) + (1.0 if own else 0.0))
        ones = jnp.ones_like(norm[0])
        for k in range(3):
            rows[base + k : base + k + 1, :] = norm[k] if own else ones
            rows[base + 3 + k : base + 4 + k, :] = ones if own else norm[k]

    @pl.loop(0, 3 * leaves)
    def _(s):
        point = centred(sites, s // leaves, lax.rem(s, leaves), leaves, centre)
        x = [wide[s, a].astype(F32) for a in range(3)]
        along = point[0] * x[0] + point[1] * x[1] + point[2] * x[2]
        norm = square(point)
        parts = [point[a] * x[b] for a in range(3) for b in range(3)]
        parts += [3.0 * point[a] * along - norm * x[a] for a in range(3)]
        for a in range(3):
            moments[s, a * vectors : (a + 1) * vectors, :] = wide[s, a]
        for k, part in enumerate(parts):
            high, low = halves(part)
            place = (3 + k) * vectors
            moments[s, place : place + vectors, :] = high
            place = (15 + k) * vectors
            moments[s, place : place + vectors, :] = low
        fill(point, -2.0, False)
        source_rows[s] = rows[...].T.astype(BF16)

    @pl.loop(0, leaves)
    def _(t):
        fill(centred(sites, 1, t, leaves, centre), 1.0, True)
        target_rows[t] = rows[...].astype(BF16)

    for t in range(leaves):
        target = target_rows[t]
        for pair in range(0, slots, 2):
            kernels, values = [], []
            for slot in range(pair, min(pair + 2, slots)):
                source = near_lists[t, slot]
                place = jnp.where(source >= 0, source - first, empty)
                site = jnp.where(source >= 0, source - first, leaves + t)
                radius = jnp.dot(source_rows[site], target, preferred_element_type=F32)
                inverse = lax.rsqrt(radius)
                weight = inverse * inverse
                kernels.append((weight * weight * inverse).astype(BF16))
                values.append(moments[place])
            term = jnp.dot(
                jnp.concatenate(values, axis=1),
                jnp.concatenate(kernels, axis=0),
                preferred_element_type=F32,
            )
            if pair == 0:
                total[...] = term
            else:
                total[...] += term

        point = centred(sites, 1, t, leaves, centre)
        norm = square(point) + 1.0
        root = jnp.sqrt(polar[pl.ds(t, 1), :])

        def group(k):
            return total[k * vectors : (k + 1) * vectors, :]

        def both(k):
            return group(3 + k) + group(15 + k)

        plain = [group(a) for a in range(3)]
        cross = [[both(3 * a + b) for b in range(3)] for a in range(3)]
        trace = cross[0][0] + cross[1][1] + cross[2][2]
        inner = point[0] * plain[0] + point[1] * plain[1] + point[2] * plain[2]
        leaf_field = wide_dot(down, leaf_transfer[t], True).astype(BF16)
        for a in range(3):
            value = 3.0 * point[a] * (inner - trace) + both(9 + a) - norm * plain[a]
            for b in range(3):
                value += point[b] * (2.0 * cross[b][a] - 3.0 * cross[a][b])
            far = jnp.dot(leaf_field, basis[t, a], preferred_element_type=F32)
            out[t, a] = ((value + far) * root).astype(BF16)


def shards(
    n,
    minor,
    probes,
    positions,
    polar,
    basis,
    leaf_transfer,
    cluster_transfer,
    upper_transfer,
    cluster_coupling,
    upper_coupling,
    near_lists,
    cluster_lists,
    upper_lists,
):
    leaves, vectors, _, leaf_size = probes.shape
    probes = jnp.transpose(probes, (0, 2, 1, 3))
    basis = jnp.transpose(basis, (0, 2, 1, 3))
    positions = jnp.transpose(positions, (1, 0, 2))
    rank = leaf_transfer.shape[1]
    site_rows = -(-3 * leaves // 8) * 8
    wide, sites, coefs = pl.pallas_call(
        functools.partial(exchange, n, minor),
        out_shape=(
            jax.ShapeDtypeStruct((3 * leaves, 3, vectors, leaf_size), BF16),
            jax.ShapeDtypeStruct((3, site_rows, leaf_size), F32),
            jax.ShapeDtypeStruct((n, vectors, 2 * rank), F32),
        ),
        in_specs=[VMEM] * 6,
        out_specs=(VMEM,) * 3,
        scratch_shapes=[
            pltpu.SemaphoreType.DMA((n,)),
            pltpu.SemaphoreType.DMA((n,)),
            pltpu.SemaphoreType.DMA((2, 2)),
            pltpu.SemaphoreType.DMA((2, 2)),
        ],
        compiler_params=pltpu.CompilerParams(
            collective_id=0, has_side_effects=True, vmem_limit_bytes=24 << 20
        ),
        name="exchange",
    )(probes, positions, polar, basis, leaf_transfer, cluster_transfer)
    groups = 27 * vectors
    applied = pl.pallas_call(
        functools.partial(apply_operator, n, minor),
        out_shape=jax.ShapeDtypeStruct((leaves, 3, vectors, leaf_size), BF16),
        in_specs=[SMEM] * 3 + [VMEM] * 10,
        out_specs=VMEM,
        scratch_shapes=[
            pltpu.VMEM((3 * leaves + 1, groups, leaf_size), BF16),
            pltpu.VMEM((3 * leaves, leaf_size, FEATURES), BF16),
            pltpu.VMEM((leaves, FEATURES, leaf_size), BF16),
            pltpu.VMEM((FEATURES, leaf_size), F32),
            pltpu.VMEM((groups, leaf_size), F32),
            pltpu.VMEM((n, vectors, rank), F32),
        ],
        compiler_params=pltpu.CompilerParams(vmem_limit_bytes=48 << 20),
        name="apply_operator",
    )(
        near_lists,
        cluster_lists,
        upper_lists.T,
        wide,
        sites,
        coefs,
        polar,
        basis,
        leaf_transfer,
        cluster_transfer,
        upper_transfer,
        cluster_coupling,
        upper_coupling,
    )
    return jnp.transpose(applied, (0, 2, 1, 3))


def solution(mesh):
    n = mesh.shape["gx"] * mesh.shape["gy"]
    split = ("groups", "gx", "gy")
    in_specs = (
        P(split, None, None, None),
        P(split, None, None),
        P(split, None),
        P(split, None, None, None),
        P(split, None, None),
        P(split, None, None),
        P("groups", None, None),
        P(split, None, None, None),
        P("groups", None, None, None),
        P(split, None),
        P(split, None),
        P("groups", None),
    )
    return jax.shard_map(
        functools.partial(shards, n, mesh.shape["gy"]),
        mesh=mesh,
        in_specs=in_specs,
        out_specs=P(split, None, None, None),
        check_vma=False,
    )
```

```python
import functools

import jax
import jax.numpy as jnp
from jax import lax
from jax.experimental import pallas as pl
from jax.experimental.pallas import tpu as pltpu
from jax.sharding import PartitionSpec as P

UP = 3
FEATURES = 128
GROUP = 2
MESH = pl.DeviceIdType.MESH
F32 = jnp.float32
BF16 = jnp.bfloat16
SMEM = pl.BlockSpec(memory_space=pltpu.SMEM)
ANY = pl.BlockSpec(memory_space=pl.ANY)


def halves(value):
    high = value.astype(BF16)
    return high, (value - high.astype(F32)).astype(BF16)


def thirds(value):
    high, rest = value.astype(BF16).astype(F32), None
    rest = value - high
    middle = rest.astype(BF16).astype(F32)
    return high, middle, (rest - middle).astype(BF16).astype(F32)


def wide_dot(value, matrix, transposed):
    rows = value.shape[0]
    both = jnp.concatenate(halves(value), axis=0)
    dims = (((1,), (1 if transposed else 0,)), ((), ()))
    out = lax.dot_general(both, matrix, dims, preferred_element_type=F32)
    return out[:rows] + out[rows:]


def centred(sites, side, leaf, leaves, centre):
    point = [sites[side, pl.ds(a * leaves + leaf, 1), :] for a in range(3)]
    return [point[0] - centre] + point[1:]


def square(point):
    return point[0] * point[0] + point[1] * point[1] + point[2] * point[2]


def apply_operator(
    n,
    minor,
    probes_hbm,
    positions_hbm,
    polar_hbm,
    basis_hbm,
    leaf_transfer_hbm,
    cluster_transfer_hbm,
    upper_transfer_hbm,
    cluster_coupling_hbm,
    upper_coupling_hbm,
    near_lists,
    cluster_lists,
    upper_lists,
    out,
    probes,
    positions,
    polar,
    basis,
    leaf_transfer,
    cluster_transfer,
    upper_transfer,
    coupling,
    wide,
    sites,
    coefs,
    moments,
    source_rows,
    target_rows,
    rows,
    total,
    level,
    load_sem,
    coupling_sem,
    coef_send,
    coef_recv,
    halo_send,
    halo_recv,
):
    leaves = probes.shape[0]
    slots = near_lists.shape[1]
    far_slots = cluster_lists.shape[1]
    vectors = wide.shape[2]
    rank = basis.shape[2]
    me = lax.axis_index("gx") * minor + lax.axis_index("gy")

    def at(device):
        return {"gx": device // minor, "gy": lax.rem(device, minor)}

    def place_of(lev):
        return n - (n >> lev - 1) + (me >> lev)

    def load(k, source, target):
        copy = pltpu.make_async_copy(source, target, load_sem.at[k])
        copy.start()
        return copy

    barrier = pltpu.get_barrier_semaphore()

    @pl.loop(1, n)
    def _(k):
        pl.semaphore_signal(
            barrier, inc=1, device_id=at(lax.rem(me + k, n)), device_id_type=MESH
        )

    first_loads = [
        load(0, polar_hbm, polar),
        load(1, probes_hbm, probes),
        load(2, positions_hbm, positions),
    ]
    basis_loads = [
        load(3, basis_hbm, basis),
        load(4, leaf_transfer_hbm, leaf_transfer),
        load(5, cluster_transfer_hbm, cluster_transfer),
    ]
    far_loads = [
        load(6, upper_transfer_hbm, upper_transfer),
        load(7, cluster_coupling_hbm.at[0], coupling.at[0]),
    ]
    for lev in range(1, UP + 1):
        copy = pltpu.make_async_copy(
            upper_coupling_hbm.at[place_of(lev)], coupling.at[lev], coupling_sem.at[lev]
        )
        copy.start()
        far_loads.append(copy)

    def coef_copy(k, source):
        return pltpu.make_async_remote_copy(
            src_ref=coefs.at[source],
            dst_ref=coefs.at[source],
            send_sem=coef_send.at[k],
            recv_sem=coef_recv.at[source],
            device_id=at(lax.rem(me + k, n)),
            device_id_type=MESH,
        )

    def halo(side, device):
        return (
            pltpu.make_async_remote_copy(
                src_ref=sites.at[1],
                dst_ref=sites.at[2 * side],
                send_sem=halo_send.at[side, 1],
                recv_sem=halo_recv.at[side, 1],
                device_id=at(device),
                device_id_type=MESH,
            ),
            pltpu.make_async_remote_copy(
                src_ref=wide.at[pl.ds(leaves, leaves)],
                dst_ref=wide.at[pl.ds(2 * leaves * side, leaves)],
                send_sem=halo_send.at[side, 0],
                recv_sem=halo_recv.at[side, 0],
                device_id=at(device),
                device_id_type=MESH,
            ),
        )

    after = lax.rem(me + 1, n)
    before = lax.rem(me + n - 1, n)

    for copy in first_loads:
        copy.wait()
    for t in range(leaves):
        root = jnp.sqrt(polar[pl.ds(t, 1), :])
        for a in range(3):
            wide[leaves + t, a] = (root * probes[t, a].astype(F32)).astype(BF16)
    sites[1] = jnp.zeros(sites.shape[1:], F32)
    for a in range(3):
        sites[1, pl.ds(a * leaves, leaves), :] = positions[a]
    pl.semaphore_wait(barrier, n - 1)

    @pl.when(me < n - 1)
    def _():
        for copy in halo(0, after):
            copy.start()

    @pl.when(me > 0)
    def _():
        for copy in halo(1, before):
            copy.start()

    for copy in basis_loads:
        copy.wait()
    cluster = None
    for t in range(leaves):
        coef = None
        for a in range(3):
            part = lax.dot_general(
                wide[leaves + t, a], basis[t, a], (((1,), (1,)), ((), ())), preferred_element_type=F32
            )
            coef = part if coef is None else coef + part
        carried = wide_dot(coef, leaf_transfer[t], False)
        cluster = carried if cluster is None else cluster + carried
    lifted = wide_dot(cluster, cluster_transfer[0], False)
    coefs[me] = jnp.concatenate([cluster, lifted], axis=1)

    @pl.loop(1, n)
    def _(k):
        coef_copy(k, me).start()

    centre = (2 * leaves * me + leaves - 1).astype(F32)
    first = (me - 1) * leaves
    empty = 3 * leaves
    rows[...] = jnp.zeros(rows.shape, F32)
    moments[empty] = jnp.zeros(moments.shape[1:], BF16)

    def fill(point, factor, own):
        base = 0
        for a in range(3):
            one, two, three = thirds(point[a] * factor)
            order = (one, one, two, two, one, three) if own else (one, two, one, two, three, one)
            for k, row in enumerate(order):
                rows[base + k : base + k + 1, :] = row
            base += 6
        norm = thirds(square(point) + (1.0 if own else 0.0))
        ones = jnp.ones_like(norm[0])
        for k in range(3):
            rows[base + k : base + k + 1, :] = norm[k] if own else ones
            rows[base + 3 + k : base + 4 + k, :] = ones if own else norm[k]

    def prepare(side, leaf):
        s = side * leaves + leaf
        point = centred(sites, side, leaf, leaves, centre)
        x = [wide[s, a].astype(F32) for a in range(3)]
        along = point[0] * x[0] + point[1] * x[1] + point[2] * x[2]
        norm = square(point)
        parts = [point[a] * x[b] for a in range(3) for b in range(3)]
        parts += [3.0 * point[a] * along - norm * x[a] for a in range(3)]
        for a in range(3):
            moments[s, a * vectors : (a + 1) * vectors, :] = wide[s, a]
        for k, part in enumerate(parts):
            high, low = halves(part)
            place = (3 + k) * vectors
            moments[s, place : place + vectors, :] = high
            place = (15 + k) * vectors
            moments[s, place : place + vectors, :] = low
        fill(point, -2.0, False)
        source_rows[s] = rows[...].T.astype(BF16)

    def kernel_matrix(site, target):
        radius = jnp.dot(source_rows[site], target, preferred_element_type=F32)
        inverse = lax.rsqrt(radius)
        weight = inverse * inverse
        return (weight * weight * inverse).astype(BF16)

    @pl.loop(0, leaves)
    def _(t):
        prepare(1, t)
        fill(centred(sites, 1, t, leaves, centre), 1.0, True)
        target_rows[t] = rows[...].astype(BF16)

    @pl.loop(0, leaves)
    def _(t):
        matrix = kernel_matrix(leaves + t, target_rows[t])
        total[t] = jnp.dot(moments[leaves + t], matrix, preferred_element_type=F32)

    for copy in far_loads:
        copy.wait()

    @pl.loop(1, n)
    def _(k):
        coef_copy(k, lax.rem(me + k, n)).wait_recv()

    for node in range(n // 2):
        level[node] = coefs[2 * node, :, rank:] + coefs[2 * node + 1, :, rank:]
    for lev in range(1, UP):
        start = n - (n >> lev - 1)
        above = n - (n >> lev)
        for node in range(n >> lev + 1):
            place = start + 2 * node
            level[above + node] = wide_dot(
                level[place], upper_transfer[place], False
            ) + wide_dot(level[place + 1], upper_transfer[place + 1], False)
    fields = []
    for lev in range(UP + 1):
        field = None
        for s in range(far_slots):
            if lev == 0:
                source = coefs[cluster_lists[0, s], :, :rank]
            else:
                source = level[n - (n >> lev - 1) + upper_lists[s, place_of(lev)]]
            term = wide_dot(source, coupling[lev, s], True)
            field = term if field is None else field + term
        fields.append(field)
    down = fields[UP]
    for lev in range(UP - 1, -1, -1):
        matrix = upper_transfer[place_of(lev)] if lev else cluster_transfer[0]
        down = fields[lev] + wide_dot(down, matrix, True)

    @pl.when(me > 0)
    def _():
        for copy in halo(0, before):
            copy.wait_recv()

    @pl.when(me < n - 1)
    def _():
        for copy in halo(1, after):
            copy.wait_recv()

    @pl.loop(0, leaves)
    def _(t):
        prepare(0, t)

    @pl.loop(0, leaves)
    def _(t):
        prepare(2, t)

    for t in range(leaves):
        target = target_rows[t]
        for begin in range(1, slots, GROUP):
            kernels, values = [], []
            for slot in range(begin, min(begin + GROUP, slots)):
                source = near_lists[t, slot]
                site = jnp.clip(source - first, 0, empty - 1)
                place = jnp.where(source >= 0, site, empty)
                kernels.append(kernel_matrix(jnp.where(source >= 0, site, leaves + t), target))
                values.append(moments[place])
            total[t] += jnp.dot(
                jnp.concatenate(values, axis=1),
                jnp.concatenate(kernels, axis=0),
                preferred_element_type=F32,
            )

        point = centred(sites, 1, t, leaves, centre)
        norm = square(point) + 1.0
        root = jnp.sqrt(polar[pl.ds(t, 1), :])

        def group(k):
            return total[t, k * vectors : (k + 1) * vectors, :]

        def both(k):
            return group(3 + k) + group(15 + k)

        plain = [group(a) for a in range(3)]
        cross = [[both(3 * a + b) for b in range(3)] for a in range(3)]
        trace = cross[0][0] + cross[1][1] + cross[2][2]
        inner = point[0] * plain[0] + point[1] * plain[1] + point[2] * plain[2]
        leaf_field = wide_dot(down, leaf_transfer[t], True).astype(BF16)
        for a in range(3):
            value = 3.0 * point[a] * (inner - trace) + both(9 + a) - norm * plain[a]
            for b in range(3):
                value += point[b] * (2.0 * cross[b][a] - 3.0 * cross[a][b])
            far = jnp.dot(leaf_field, basis[t, a], preferred_element_type=F32)
            out[t, a] = ((value + far) * root).astype(BF16)

    @pl.loop(1, n)
    def _(k):
        coef_copy(k, me).wait_send()

    @pl.when(me < n - 1)
    def _():
        for copy in halo(0, after):
            copy.wait_send()

    @pl.when(me > 0)
    def _():
        for copy in halo(1, before):
            copy.wait_send()


def shards(
    n,
    minor,
    probes,
    positions,
    polar,
    basis,
    leaf_transfer,
    cluster_transfer,
    upper_transfer,
    cluster_coupling,
    upper_coupling,
    near_lists,
    cluster_lists,
    upper_lists,
):
    leaves, vectors, _, leaf_size = probes.shape
    probes = jnp.transpose(probes, (0, 2, 1, 3))
    basis = jnp.transpose(basis, (0, 2, 1, 3))
    positions = jnp.transpose(positions, (1, 0, 2))
    rank = leaf_transfer.shape[1]
    site_rows = -(-3 * leaves // 8) * 8
    groups = 27 * vectors
    slots = cluster_coupling.shape[1]

    def like(array):
        return pltpu.VMEM(array.shape, array.dtype)

    applied = pl.pallas_call(
        functools.partial(apply_operator, n, minor),
        out_shape=jax.ShapeDtypeStruct((leaves, 3, vectors, leaf_size), BF16),
        in_specs=[ANY] * 9 + [SMEM] * 3,
        out_specs=pl.BlockSpec(memory_space=pltpu.VMEM),
        scratch_shapes=[
            like(probes),
            like(positions),
            like(polar),
            like(basis),
            like(leaf_transfer),
            like(cluster_transfer),
            like(upper_transfer),
            pltpu.VMEM((UP + 1, slots, rank, rank), BF16),
            pltpu.VMEM((3 * leaves, 3, vectors, leaf_size), BF16),
            pltpu.VMEM((3, site_rows, leaf_size), F32),
            pltpu.VMEM((n, vectors, 2 * rank), F32),
            pltpu.VMEM((3 * leaves + 1, groups, leaf_size), BF16),
            pltpu.VMEM((3 * leaves, leaf_size, FEATURES), BF16),
            pltpu.VMEM((leaves, FEATURES, leaf_size), BF16),
            pltpu.VMEM((FEATURES, leaf_size), F32),
            pltpu.VMEM((leaves, groups, leaf_size), F32),
            pltpu.VMEM((n, vectors, rank), F32),
            pltpu.SemaphoreType.DMA((8,)),
            pltpu.SemaphoreType.DMA((UP + 1,)),
            pltpu.SemaphoreType.DMA((n,)),
            pltpu.SemaphoreType.DMA((n,)),
            pltpu.SemaphoreType.DMA((2, 2)),
            pltpu.SemaphoreType.DMA((2, 2)),
        ],
        compiler_params=pltpu.CompilerParams(
            collective_id=0, has_side_effects=True, vmem_limit_bytes=56 << 20
        ),
        name="apply_operator",
    )(
        probes,
        positions,
        polar,
        basis,
        leaf_transfer,
        cluster_transfer,
        upper_transfer,
        cluster_coupling,
        upper_coupling,
        near_lists,
        cluster_lists,
        upper_lists.T,
    )
    return jnp.transpose(applied, (0, 2, 1, 3))


def solution(mesh):
    n = mesh.shape["gx"] * mesh.shape["gy"]
    split = ("groups", "gx", "gy")
    in_specs = (
        P(split, None, None, None),
        P(split, None, None),
        P(split, None),
        P(split, None, None, None),
        P(split, None, None),
        P(split, None, None),
        P("groups", None, None),
        P(split, None, None, None),
        P("groups", None, None, None),
        P(split, None),
        P(split, None),
        P("groups", None),
    )
    return jax.shard_map(
        functools.partial(shards, n, mesh.shape["gy"]),
        mesh=mesh,
        in_specs=in_specs,
        out_specs=P(split, None, None, None),
        check_vma=False,
    )
```

```python
import functools

import jax
import jax.numpy as jnp
from jax import lax
from jax.experimental import pallas as pl
from jax.experimental.pallas import tpu as pltpu
from jax.sharding import PartitionSpec as P

UP = 3
FEATURES = 128
MESH = pl.DeviceIdType.MESH
F32 = jnp.float32
BF16 = jnp.bfloat16
ANY = pl.BlockSpec(memory_space=pl.ANY)


def halves(value):
    high = value.astype(BF16)
    return high, (value - high.astype(F32)).astype(BF16)


def thirds(value):
    high, rest = value.astype(BF16).astype(F32), None
    rest = value - high
    middle = rest.astype(BF16).astype(F32)
    return high, middle, (rest - middle).astype(BF16).astype(F32)


def wide_dot(value, matrix, transposed):
    rows = value.shape[0]
    both = jnp.concatenate(halves(value), axis=0)
    dims = (((1,), (1 if transposed else 0,)), ((), ()))
    out = lax.dot_general(both, matrix, dims, preferred_element_type=F32)
    return out[:rows] + out[rows:]


def centred(sites, side, leaf, leaves, centre):
    point = [sites[side, pl.ds(a * leaves + leaf, 1), :] for a in range(3)]
    return [point[0] - centre] + point[1:]


def square(point):
    return point[0] * point[0] + point[1] * point[1] + point[2] * point[2]


def apply_operator(
    n,
    minor,
    probes_hbm,
    positions_hbm,
    polar_hbm,
    basis_hbm,
    leaf_transfer_hbm,
    cluster_transfer_hbm,
    upper_transfer_hbm,
    cluster_coupling_hbm,
    upper_coupling_hbm,
    near_lists_hbm,
    cluster_lists_hbm,
    upper_lists_hbm,
    out,
    probes,
    positions,
    polar,
    basis,
    leaf_transfer,
    cluster_transfer,
    upper_transfer,
    coupling,
    wide,
    sites,
    coefs,
    moments,
    source_rows,
    target_rows,
    rows,
    total,
    matrices,
    level,
    near_lists,
    cluster_lists,
    upper_lists,
    load_sem,
    coupling_sem,
    coef_send,
    coef_recv,
    halo_send,
    halo_recv,
):
    leaves = probes.shape[0]
    slots = near_lists.shape[1]
    far_slots = cluster_lists.shape[1]
    vectors = wide.shape[2]
    leaf_size = wide.shape[3]
    rank = basis.shape[2]
    me = lax.axis_index("gx") * minor + lax.axis_index("gy")

    def at(device):
        return {"gx": device // minor, "gy": lax.rem(device, minor)}

    def place_of(lev):
        return n - (n >> lev - 1) + (me >> lev)

    def load(k, source, target):
        copy = pltpu.make_async_copy(source, target, load_sem.at[k])
        copy.start()
        return copy

    barrier = pltpu.get_barrier_semaphore()

    @pl.loop(1, n)
    def _(k):
        pl.semaphore_signal(
            barrier, inc=1, device_id=at(lax.rem(me + k, n)), device_id_type=MESH
        )

    first_loads = [
        load(2, positions_hbm, positions),
        load(0, polar_hbm, polar),
        load(1, probes_hbm, probes),
    ]
    basis_loads = [
        load(3, basis_hbm, basis),
        load(4, leaf_transfer_hbm, leaf_transfer),
        load(5, cluster_transfer_hbm, cluster_transfer),
    ]
    list_loads = [
        load(8, near_lists_hbm, near_lists),
        load(9, cluster_lists_hbm, cluster_lists),
        load(10, upper_lists_hbm, upper_lists),
    ]
    far_loads = [
        load(6, upper_transfer_hbm, upper_transfer),
        load(7, cluster_coupling_hbm.at[0], coupling.at[0]),
    ]
    for lev in range(1, UP + 1):
        copy = pltpu.make_async_copy(
            upper_coupling_hbm.at[place_of(lev)], coupling.at[lev], coupling_sem.at[lev]
        )
        copy.start()
        far_loads.append(copy)

    def coef_copy(k, source):
        return pltpu.make_async_remote_copy(
            src_ref=coefs.at[source],
            dst_ref=coefs.at[source],
            send_sem=coef_send.at[k],
            recv_sem=coef_recv.at[source],
            device_id=at(lax.rem(me + k, n)),
            device_id_type=MESH,
        )

    def halo(side, device):
        return (
            pltpu.make_async_remote_copy(
                src_ref=sites.at[1],
                dst_ref=sites.at[2 * side],
                send_sem=halo_send.at[side, 1],
                recv_sem=halo_recv.at[side, 1],
                device_id=at(device),
                device_id_type=MESH,
            ),
            pltpu.make_async_remote_copy(
                src_ref=wide.at[pl.ds(leaves, leaves)],
                dst_ref=wide.at[pl.ds(2 * leaves * side, leaves)],
                send_sem=halo_send.at[side, 0],
                recv_sem=halo_recv.at[side, 0],
                device_id=at(device),
                device_id_type=MESH,
            ),
        )

    after = lax.rem(me + 1, n)
    before = lax.rem(me + n - 1, n)

    first_loads[0].wait()
    sites[1] = jnp.zeros(sites.shape[1:], F32)
    for a in range(3):
        sites[1, pl.ds(a * leaves, leaves), :] = positions[a]
    for copy in first_loads[1:]:
        copy.wait()
    for t in range(leaves):
        root = jnp.sqrt(polar[pl.ds(t, 1), :])
        for a in range(3):
            wide[leaves + t, a] = (root * probes[t, a].astype(F32)).astype(BF16)
    pl.semaphore_wait(barrier, n - 1)

    @pl.when(me < n - 1)
    def _():
        for copy in halo(0, after):
            copy.start()

    @pl.when(me > 0)
    def _():
        for copy in halo(1, before):
            copy.start()

    for copy in basis_loads:
        copy.wait()
    cluster = None
    for t in range(leaves):
        coef = None
        for a in range(3):
            part = lax.dot_general(
                wide[leaves + t, a], basis[t, a], (((1,), (1,)), ((), ())), preferred_element_type=F32
            )
            coef = part if coef is None else coef + part
        carried = wide_dot(coef, leaf_transfer[t], False)
        cluster = carried if cluster is None else cluster + carried
    lifted = wide_dot(cluster, cluster_transfer[0], False)
    coefs[me] = jnp.concatenate([cluster, lifted], axis=1)

    @pl.loop(1, n)
    def _(k):
        coef_copy(k, me).start()

    centre = (2 * leaves * me + leaves - 1).astype(F32)
    first = (me - 1) * leaves
    empty = 3 * leaves
    rows[...] = jnp.zeros(rows.shape, F32)
    moments[empty] = jnp.zeros(moments.shape[1:], BF16)

    def fill(point, factor, own):
        base = 0
        for a in range(3):
            one, two, three = thirds(point[a] * factor)
            order = (one, one, two, two, one, three) if own else (one, two, one, two, three, one)
            for k, row in enumerate(order):
                rows[base + k : base + k + 1, :] = row
            base += 6
        norm = thirds(square(point) + (1.0 if own else 0.0))
        ones = jnp.ones_like(norm[0])
        for k in range(3):
            rows[base + k : base + k + 1, :] = norm[k] if own else ones
            rows[base + 3 + k : base + 4 + k, :] = ones if own else norm[k]

    def prepare(side, leaf):
        s = side * leaves + leaf
        point = centred(sites, side, leaf, leaves, centre)
        x = [wide[s, a].astype(F32) for a in range(3)]
        along = point[0] * x[0] + point[1] * x[1] + point[2] * x[2]
        norm = square(point)
        parts = [point[a] * x[b] for a in range(3) for b in range(3)]
        parts += [3.0 * point[a] * along - norm * x[a] for a in range(3)]
        for a in range(3):
            moments[s, a * vectors : (a + 1) * vectors, :] = wide[s, a]
        for k, part in enumerate(parts):
            high, low = halves(part)
            place = (3 + k) * vectors
            moments[s, place : place + vectors, :] = high
            place = (15 + k) * vectors
            moments[s, place : place + vectors, :] = low

    def prepare_rows(side, leaf):
        fill(centred(sites, side, leaf, leaves, centre), -2.0, False)
        source_rows[side * leaves + leaf] = rows[...].T.astype(BF16)

    def kernel_matrix(site, target):
        radius = jnp.dot(source_rows[site], target, preferred_element_type=F32)
        inverse = lax.rsqrt(radius)
        weight = inverse * inverse
        return (weight * weight * inverse).astype(BF16)

    @pl.loop(0, leaves)
    def _(t):
        prepare(1, t)
        prepare_rows(1, t)
        fill(centred(sites, 1, t, leaves, centre), 1.0, True)
        target_rows[t] = rows[...].astype(BF16)

    @pl.loop(0, leaves)
    def _(t):
        matrix = kernel_matrix(leaves + t, target_rows[t])
        total[t] = jnp.dot(moments[leaves + t], matrix, preferred_element_type=F32)

    @pl.when(me > 0)
    def _():
        halo(0, before)[0].wait_recv()

    @pl.when(me < n - 1)
    def _():
        halo(1, after)[0].wait_recv()

    for copy in list_loads:
        copy.wait()

    @pl.loop(0, leaves)
    def _(t):
        prepare_rows(0, t)
        prepare_rows(2, t)

    def site_of(t, slot):
        source = near_lists[t, slot]
        return source, jnp.clip(source - first, 0, empty - 1)

    @pl.loop(0, leaves)
    def _(t):
        target = target_rows[t]
        for slot in range(1, slots):
            source, site = site_of(t, slot)
            block = kernel_matrix(jnp.where(source >= 0, site, leaves + t), target)
            matrices[t, (slot - 1) * leaf_size : slot * leaf_size, :] = block

    for copy in far_loads:
        copy.wait()

    @pl.loop(1, n)
    def _(k):
        coef_copy(k, lax.rem(me + k, n)).wait_recv()

    for node in range(n // 2):
        level[node] = coefs[2 * node, :, rank:] + coefs[2 * node + 1, :, rank:]
    for lev in range(1, UP):
        start = n - (n >> lev - 1)
        above = n - (n >> lev)
        for node in range(n >> lev + 1):
            place = start + 2 * node
            level[above + node] = wide_dot(
                level[place], upper_transfer[place], False
            ) + wide_dot(level[place + 1], upper_transfer[place + 1], False)
    fields = []
    for lev in range(UP + 1):
        field = None
        for s in range(far_slots):
            if lev == 0:
                source = coefs[cluster_lists[0, s], :, :rank]
            else:
                source = level[n - (n >> lev - 1) + upper_lists[s, place_of(lev)]]
            term = wide_dot(source, coupling[lev, s], True)
            field = term if field is None else field + term
        fields.append(field)
    down = fields[UP]
    for lev in range(UP - 1, -1, -1):
        matrix = upper_transfer[place_of(lev)] if lev else cluster_transfer[0]
        down = fields[lev] + wide_dot(down, matrix, True)

    @pl.when(me > 0)
    def _():
        halo(0, before)[1].wait_recv()

    @pl.when(me < n - 1)
    def _():
        halo(1, after)[1].wait_recv()

    @pl.loop(0, leaves)
    def _(t):
        prepare(0, t)
        prepare(2, t)

    for t in range(leaves):
        values = []
        for slot in range(1, slots):
            source, site = site_of(t, slot)
            values.append(moments[jnp.where(source >= 0, site, empty)])
        total[t] += jnp.dot(
            jnp.concatenate(values, axis=1), matrices[t], preferred_element_type=F32
        )

        point = centred(sites, 1, t, leaves, centre)
        norm = square(point) + 1.0
        root = jnp.sqrt(polar[pl.ds(t, 1), :])

        def group(k):
            return total[t, k * vectors : (k + 1) * vectors, :]

        def both(k):
            return group(3 + k) + group(15 + k)

        plain = [group(a) for a in range(3)]
        cross = [[both(3 * a + b) for b in range(3)] for a in range(3)]
        trace = cross[0][0] + cross[1][1] + cross[2][2]
        inner = point[0] * plain[0] + point[1] * plain[1] + point[2] * plain[2]
        leaf_field = wide_dot(down, leaf_transfer[t], True).astype(BF16)
        for a in range(3):
            value = 3.0 * point[a] * (inner - trace) + both(9 + a) - norm * plain[a]
            for b in range(3):
                value += point[b] * (2.0 * cross[b][a] - 3.0 * cross[a][b])
            far = jnp.dot(leaf_field, basis[t, a], preferred_element_type=F32)
            out[t, a] = ((value + far) * root).astype(BF16)

    @pl.loop(1, n)
    def _(k):
        coef_copy(k, me).wait_send()

    @pl.when(me < n - 1)
    def _():
        for copy in halo(0, after):
            copy.wait_send()

    @pl.when(me > 0)
    def _():
        for copy in halo(1, before):
            copy.wait_send()


def shards(
    n,
    minor,
    probes,
    positions,
    polar,
    basis,
    leaf_transfer,
    cluster_transfer,
    upper_transfer,
    cluster_coupling,
    upper_coupling,
    near_lists,
    cluster_lists,
    upper_lists,
):
    leaves, vectors, _, leaf_size = probes.shape
    probes = jnp.transpose(probes, (0, 2, 1, 3))
    basis = jnp.transpose(basis, (0, 2, 1, 3))
    positions = jnp.transpose(positions, (1, 0, 2))
    rank = leaf_transfer.shape[1]
    site_rows = -(-3 * leaves // 8) * 8
    groups = 27 * vectors
    slots = cluster_coupling.shape[1]

    def like(array):
        return pltpu.VMEM(array.shape, array.dtype)

    applied = pl.pallas_call(
        functools.partial(apply_operator, n, minor),
        out_shape=jax.ShapeDtypeStruct((leaves, 3, vectors, leaf_size), BF16),
        in_specs=[ANY] * 12,
        out_specs=pl.BlockSpec(memory_space=pltpu.VMEM),
        scratch_shapes=[
            like(probes),
            like(positions),
            like(polar),
            like(basis),
            like(leaf_transfer),
            like(cluster_transfer),
            like(upper_transfer),
            pltpu.VMEM((UP + 1, slots, rank, rank), BF16),
            pltpu.VMEM((3 * leaves, 3, vectors, leaf_size), BF16),
            pltpu.VMEM((3, site_rows, leaf_size), F32),
            pltpu.VMEM((n, vectors, 2 * rank), F32),
            pltpu.VMEM((3 * leaves + 1, groups, leaf_size), BF16),
            pltpu.VMEM((3 * leaves, leaf_size, FEATURES), BF16),
            pltpu.VMEM((leaves, FEATURES, leaf_size), BF16),
            pltpu.VMEM((FEATURES, leaf_size), F32),
            pltpu.VMEM((leaves, groups, leaf_size), F32),
            pltpu.VMEM((leaves, (near_lists.shape[1] - 1) * leaf_size, leaf_size), BF16),
            pltpu.VMEM((n, vectors, rank), F32),
            pltpu.SMEM(near_lists.shape, jnp.int32),
            pltpu.SMEM(cluster_lists.shape, jnp.int32),
            pltpu.SMEM(upper_lists.shape[::-1], jnp.int32),
            pltpu.SemaphoreType.DMA((11,)),
            pltpu.SemaphoreType.DMA((UP + 1,)),
            pltpu.SemaphoreType.DMA((n,)),
            pltpu.SemaphoreType.DMA((n,)),
            pltpu.SemaphoreType.DMA((2, 2)),
            pltpu.SemaphoreType.DMA((2, 2)),
        ],
        compiler_params=pltpu.CompilerParams(
            collective_id=0, has_side_effects=True, vmem_limit_bytes=56 << 20
        ),
        name="apply_operator",
    )(
        probes,
        positions,
        polar,
        basis,
        leaf_transfer,
        cluster_transfer,
        upper_transfer,
        cluster_coupling,
        upper_coupling,
        near_lists,
        cluster_lists,
        upper_lists.T,
    )
    return jnp.transpose(applied, (0, 2, 1, 3))


def solution(mesh):
    n = mesh.shape["gx"] * mesh.shape["gy"]
    split = ("groups", "gx", "gy")
    in_specs = (
        P(split, None, None, None),
        P(split, None, None),
        P(split, None),
        P(split, None, None, None),
        P(split, None, None),
        P(split, None, None),
        P("groups", None, None),
        P(split, None, None, None),
        P("groups", None, None, None),
        P(split, None),
        P(split, None),
        P("groups", None),
    )
    return jax.shard_map(
        functools.partial(shards, n, mesh.shape["gy"]),
        mesh=mesh,
        in_specs=in_specs,
        out_specs=P(split, None, None, None),
        check_vma=False,
    )
```

```python
import functools

import jax
import jax.numpy as jnp
from jax import lax
from jax.experimental import pallas as pl
from jax.experimental.pallas import tpu as pltpu
from jax.sharding import PartitionSpec as P

UP = 3
FEATURES = 128
USED = 32
MESH = pl.DeviceIdType.MESH
F32 = jnp.float32
BF16 = jnp.bfloat16
ANY = pl.BlockSpec(memory_space=pl.ANY)


def halves(value):
    high = value.astype(BF16)
    return high, (value - high.astype(F32)).astype(BF16)


def thirds(value):
    high, rest = value.astype(BF16).astype(F32), None
    rest = value - high
    middle = rest.astype(BF16).astype(F32)
    return high, middle, (rest - middle).astype(BF16).astype(F32)


def wide_dot(value, matrix, transposed):
    rows = value.shape[0]
    both = jnp.concatenate(halves(value), axis=0)
    dims = (((1,), (1 if transposed else 0,)), ((), ()))
    out = lax.dot_general(both, matrix, dims, preferred_element_type=F32)
    return out[:rows] + out[rows:]


def centred(positions, side, leaf, centre):
    point = [positions[side, a, pl.ds(leaf, 1), :] for a in range(3)]
    return [point[0] - centre] + point[1:]


def square(point):
    return point[0] * point[0] + point[1] * point[1] + point[2] * point[2]


def apply_operator(
    n,
    minor,
    probes_hbm,
    positions_hbm,
    polar_hbm,
    basis_hbm,
    leaf_transfer_hbm,
    cluster_transfer_hbm,
    upper_transfer_hbm,
    cluster_coupling_hbm,
    upper_coupling_hbm,
    near_lists_hbm,
    cluster_lists_hbm,
    upper_lists_hbm,
    out,
    probes,
    positions,
    polar,
    basis,
    leaf_transfer,
    cluster_transfer,
    upper_transfer,
    coupling,
    wide,
    coefs,
    moments,
    source_rows,
    target_rows,
    rows,
    total,
    matrices,
    level,
    near_lists,
    cluster_lists,
    upper_lists,
    load_sem,
    coupling_sem,
    coef_send,
    coef_recv,
    halo_send,
    halo_recv,
):
    leaves = probes.shape[1]
    slots = near_lists.shape[1]
    far_slots = cluster_lists.shape[1]
    vectors = wide.shape[2]
    leaf_size = wide.shape[3]
    rank = basis.shape[2]
    me = lax.axis_index("gx") * minor + lax.axis_index("gy")

    def at(device):
        return {"gx": device // minor, "gy": lax.rem(device, minor)}

    def place_of(lev):
        return n - (n >> lev - 1) + (me >> lev)

    def load(k, source, target):
        copy = pltpu.make_async_copy(source, target, load_sem.at[k])
        copy.start()
        return copy

    barrier = pltpu.get_barrier_semaphore()

    @pl.loop(1, n)
    def _(k):
        pl.semaphore_signal(
            barrier, inc=1, device_id=at(lax.rem(me + k, n)), device_id_type=MESH
        )

    first_loads = [
        load(2, positions_hbm, positions.at[1]),
        load(0, polar_hbm, polar.at[1]),
        load(1, probes_hbm, probes.at[1]),
    ]
    basis_loads = [
        load(3, basis_hbm, basis),
        load(4, leaf_transfer_hbm, leaf_transfer),
        load(5, cluster_transfer_hbm, cluster_transfer),
    ]
    list_loads = [
        load(8, near_lists_hbm, near_lists),
        load(9, cluster_lists_hbm, cluster_lists),
        load(10, upper_lists_hbm, upper_lists),
    ]
    far_loads = [
        load(6, upper_transfer_hbm, upper_transfer),
        load(7, cluster_coupling_hbm.at[0], coupling.at[0]),
    ]
    for lev in range(1, UP + 1):
        copy = pltpu.make_async_copy(
            upper_coupling_hbm.at[place_of(lev)], coupling.at[lev], coupling_sem.at[lev]
        )
        copy.start()
        far_loads.append(copy)

    def coef_copy(k, source):
        return pltpu.make_async_remote_copy(
            src_ref=coefs.at[source],
            dst_ref=coefs.at[source],
            send_sem=coef_send.at[k],
            recv_sem=coef_recv.at[source],
            device_id=at(lax.rem(me + k, n)),
            device_id_type=MESH,
        )

    def halo(side, part, device):
        source, target = (
            (positions_hbm, positions),
            (polar_hbm, polar),
            (probes_hbm, probes),
        )[part]
        return pltpu.make_async_remote_copy(
            src_ref=source,
            dst_ref=target.at[2 * side],
            send_sem=halo_send.at[side, part],
            recv_sem=halo_recv.at[side, part],
            device_id=at(device),
            device_id_type=MESH,
        )

    after = lax.rem(me + 1, n)
    before = lax.rem(me + n - 1, n)

    rows[...] = jnp.zeros(rows.shape, F32)
    source_rows[...] = jnp.zeros(source_rows.shape, BF16)
    moments[3 * leaves] = jnp.zeros(moments.shape[1:], BF16)
    pl.semaphore_wait(barrier, n - 1)

    @pl.when(me < n - 1)
    def _():
        for part in range(3):
            halo(0, part, after).start()

    @pl.when(me > 0)
    def _():
        for part in range(3):
            halo(1, part, before).start()

    for copy in first_loads:
        copy.wait()

    def scaled_probes(side, leaf):
        root = jnp.sqrt(polar[side, pl.ds(leaf, 1), :])
        return [(root * probes[side, leaf, a].astype(F32)).astype(BF16) for a in range(3)]

    for t in range(leaves):
        for a, value in enumerate(scaled_probes(1, t)):
            wide[t, a] = value

    for copy in basis_loads:
        copy.wait()
    cluster = None
    for t in range(leaves):
        coef = None
        for a in range(3):
            part = lax.dot_general(
                wide[t, a], basis[t, a], (((1,), (1,)), ((), ())), preferred_element_type=F32
            )
            coef = part if coef is None else coef + part
        carried = wide_dot(coef, leaf_transfer[t], False)
        cluster = carried if cluster is None else cluster + carried
    lifted = wide_dot(cluster, cluster_transfer[0], False)
    coefs[me] = jnp.concatenate([cluster, lifted], axis=1)

    @pl.loop(1, n)
    def _(k):
        coef_copy(k, me).start()

    centre = (2 * leaves * me + leaves - 1).astype(F32)
    first = (me - 1) * leaves
    empty = 3 * leaves

    def fill(point, factor, own):
        base = 0
        for a in range(3):
            one, two, three = thirds(point[a] * factor)
            order = (one, one, two, two, one, three) if own else (one, two, one, two, three, one)
            for k, row in enumerate(order):
                rows[base + k : base + k + 1, :] = row
            base += 6
        norm = thirds(square(point) + (1.0 if own else 0.0))
        ones = jnp.ones_like(norm[0])
        for k in range(3):
            rows[base + k : base + k + 1, :] = norm[k] if own else ones
            rows[base + 3 + k : base + 4 + k, :] = ones if own else norm[k]

    def prepare(side, leaf):
        s = side * leaves + leaf
        point = centred(positions, side, leaf, centre)
        held = scaled_probes(side, leaf) if side != 1 else [wide[leaf, a] for a in range(3)]
        x = [held[a].astype(F32) for a in range(3)]
        along = point[0] * x[0] + point[1] * x[1] + point[2] * x[2]
        norm = square(point)
        parts = [point[a] * x[b] for a in range(3) for b in range(3)]
        parts += [3.0 * point[a] * along - norm * x[a] for a in range(3)]
        for a in range(3):
            moments[s, a * vectors : (a + 1) * vectors, :] = held[a]
        for k, part in enumerate(parts):
            high, low = halves(part)
            place = (3 + k) * vectors
            moments[s, place : place + vectors, :] = high
            place = (15 + k) * vectors
            moments[s, place : place + vectors, :] = low

    def prepare_rows(side, leaf):
        fill(centred(positions, side, leaf, centre), -2.0, False)
        source_rows[side * leaves + leaf, :, :USED] = rows[:USED, :].T.astype(BF16)

    def kernel_matrix(site, target):
        radius = jnp.dot(source_rows[site], target, preferred_element_type=F32)
        inverse = lax.rsqrt(radius)
        weight = inverse * inverse
        return (weight * weight * inverse).astype(BF16)

    @pl.loop(0, leaves)
    def _(t):
        prepare(1, t)
        prepare_rows(1, t)
        fill(centred(positions, 1, t, centre), 1.0, True)
        target_rows[t] = rows[...].astype(BF16)

    @pl.loop(0, leaves)
    def _(t):
        matrix = kernel_matrix(leaves + t, target_rows[t])
        total[t] = jnp.dot(moments[leaves + t], matrix, preferred_element_type=F32)

    @pl.when(me > 0)
    def _():
        halo(0, 0, before).wait_recv()

    @pl.when(me < n - 1)
    def _():
        halo(1, 0, after).wait_recv()

    for copy in list_loads:
        copy.wait()

    @pl.loop(0, leaves)
    def _(t):
        prepare_rows(0, t)
        prepare_rows(2, t)

    def site_of(t, slot):
        source = near_lists[t, slot]
        return source, jnp.clip(source - first, 0, empty - 1)

    @pl.loop(0, leaves)
    def _(t):
        target = target_rows[t]
        for slot in range(1, slots):
            source, site = site_of(t, slot)
            block = kernel_matrix(jnp.where(source >= 0, site, leaves + t), target)
            matrices[t, (slot - 1) * leaf_size : slot * leaf_size, :] = block

    for copy in far_loads:
        copy.wait()

    @pl.loop(1, n)
    def _(k):
        coef_copy(k, lax.rem(me + k, n)).wait_recv()

    for node in range(n // 2):
        level[node] = coefs[2 * node, :, rank:] + coefs[2 * node + 1, :, rank:]
    for lev in range(1, UP):
        start = n - (n >> lev - 1)
        above = n - (n >> lev)
        for node in range(n >> lev + 1):
            place = start + 2 * node
            level[above + node] = wide_dot(
                level[place], upper_transfer[place], False
            ) + wide_dot(level[place + 1], upper_transfer[place + 1], False)
    fields = []
    for lev in range(UP + 1):
        field = None
        for s in range(far_slots):
            if lev == 0:
                source = coefs[cluster_lists[0, s], :, :rank]
            else:
                source = level[n - (n >> lev - 1) + upper_lists[s, place_of(lev)]]
            term = wide_dot(source, coupling[lev, s], True)
            field = term if field is None else field + term
        fields.append(field)
    down = fields[UP]
    for lev in range(UP - 1, -1, -1):
        matrix = upper_transfer[place_of(lev)] if lev else cluster_transfer[0]
        down = fields[lev] + wide_dot(down, matrix, True)

    @pl.when(me > 0)
    def _():
        for part in (1, 2):
            halo(0, part, before).wait_recv()

    @pl.when(me < n - 1)
    def _():
        for part in (1, 2):
            halo(1, part, after).wait_recv()

    @pl.loop(0, leaves)
    def _(t):
        prepare(0, t)
        prepare(2, t)

    for t in range(leaves):
        values = []
        for slot in range(1, slots):
            source, site = site_of(t, slot)
            values.append(moments[jnp.where(source >= 0, site, empty)])
        total[t] += jnp.dot(
            jnp.concatenate(values, axis=1), matrices[t], preferred_element_type=F32
        )

        point = centred(positions, 1, t, centre)
        norm = square(point) + 1.0
        root = jnp.sqrt(polar[1, pl.ds(t, 1), :])

        def group(k):
            return total[t, k * vectors : (k + 1) * vectors, :]

        def both(k):
            return group(3 + k) + group(15 + k)

        plain = [group(a) for a in range(3)]
        cross = [[both(3 * a + b) for b in range(3)] for a in range(3)]
        trace = cross[0][0] + cross[1][1] + cross[2][2]
        inner = point[0] * plain[0] + point[1] * plain[1] + point[2] * plain[2]
        leaf_field = wide_dot(down, leaf_transfer[t], True).astype(BF16)
        for a in range(3):
            value = 3.0 * point[a] * (inner - trace) + both(9 + a) - norm * plain[a]
            for b in range(3):
                value += point[b] * (2.0 * cross[b][a] - 3.0 * cross[a][b])
            far = jnp.dot(leaf_field, basis[t, a], preferred_element_type=F32)
            out[t, a] = ((value + far) * root).astype(BF16)

    @pl.loop(1, n)
    def _(k):
        coef_copy(k, me).wait_send()

    @pl.when(me < n - 1)
    def _():
        for part in range(3):
            halo(0, part, after).wait_send()

    @pl.when(me > 0)
    def _():
        for part in range(3):
            halo(1, part, before).wait_send()


def shards(
    n,
    minor,
    probes,
    positions,
    polar,
    basis,
    leaf_transfer,
    cluster_transfer,
    upper_transfer,
    cluster_coupling,
    upper_coupling,
    near_lists,
    cluster_lists,
    upper_lists,
):
    leaves, vectors, _, leaf_size = probes.shape
    probes = jnp.transpose(probes, (0, 2, 1, 3))
    basis = jnp.transpose(basis, (0, 2, 1, 3))
    positions = jnp.transpose(positions, (1, 0, 2))
    rank = leaf_transfer.shape[1]
    groups = 27 * vectors
    slots = cluster_coupling.shape[1]

    def like(array):
        return pltpu.VMEM(array.shape, array.dtype)

    applied = pl.pallas_call(
        functools.partial(apply_operator, n, minor),
        out_shape=jax.ShapeDtypeStruct((leaves, 3, vectors, leaf_size), BF16),
        in_specs=[ANY] * 12,
        out_specs=pl.BlockSpec(memory_space=pltpu.VMEM),
        scratch_shapes=[
            pltpu.VMEM((3, *probes.shape), BF16),
            pltpu.VMEM((3, *positions.shape), F32),
            pltpu.VMEM((3, *polar.shape), F32),
            like(basis),
            like(leaf_transfer),
            like(cluster_transfer),
            like(upper_transfer),
            pltpu.VMEM((UP + 1, slots, rank, rank), BF16),
            like(probes),
            pltpu.VMEM((n, vectors, 2 * rank), F32),
            pltpu.VMEM((3 * leaves + 1, groups, leaf_size), BF16),
            pltpu.VMEM((3 * leaves, leaf_size, FEATURES), BF16),
            pltpu.VMEM((leaves, FEATURES, leaf_size), BF16),
            pltpu.VMEM((FEATURES, leaf_size), F32),
            pltpu.VMEM((leaves, groups, leaf_size), F32),
            pltpu.VMEM((leaves, (near_lists.shape[1] - 1) * leaf_size, leaf_size), BF16),
            pltpu.VMEM((n, vectors, rank), F32),
            pltpu.SMEM(near_lists.shape, jnp.int32),
            pltpu.SMEM(cluster_lists.shape, jnp.int32),
            pltpu.SMEM(upper_lists.shape[::-1], jnp.int32),
            pltpu.SemaphoreType.DMA((11,)),
            pltpu.SemaphoreType.DMA((UP + 1,)),
            pltpu.SemaphoreType.DMA((n,)),
            pltpu.SemaphoreType.DMA((n,)),
            pltpu.SemaphoreType.DMA((2, 3)),
            pltpu.SemaphoreType.DMA((2, 3)),
        ],
        compiler_params=pltpu.CompilerParams(
            collective_id=0, has_side_effects=True, vmem_limit_bytes=56 << 20
        ),
        name="apply_operator",
    )(
        probes,
        positions,
        polar,
        basis,
        leaf_transfer,
        cluster_transfer,
        upper_transfer,
        cluster_coupling,
        upper_coupling,
        near_lists,
        cluster_lists,
        upper_lists.T,
    )
    return jnp.transpose(applied, (0, 2, 1, 3))


def solution(mesh):
    n = mesh.shape["gx"] * mesh.shape["gy"]
    split = ("groups", "gx", "gy")
    in_specs = (
        P(split, None, None, None),
        P(split, None, None),
        P(split, None),
        P(split, None, None, None),
        P(split, None, None),
        P(split, None, None),
        P("groups", None, None),
        P(split, None, None, None),
        P("groups", None, None, None),
        P(split, None),
        P(split, None),
        P("groups", None),
    )
    return jax.shard_map(
        functools.partial(shards, n, mesh.shape["gy"]),
        mesh=mesh,
        in_specs=in_specs,
        out_specs=P(split, None, None, None),
        check_vma=False,
    )
```

```python
import functools

import jax
import jax.numpy as jnp
from jax import lax
from jax.experimental import pallas as pl
from jax.experimental.pallas import tpu as pltpu
from jax.sharding import PartitionSpec as P

UP = 3
FEATURES = 128
USED = 32
MESH = pl.DeviceIdType.MESH
F32 = jnp.float32
BF16 = jnp.bfloat16
ANY = pl.BlockSpec(memory_space=pl.ANY)


def halves(value):
    high = value.astype(BF16)
    return high, (value - high.astype(F32)).astype(BF16)


def thirds(value):
    high, rest = value.astype(BF16).astype(F32), None
    rest = value - high
    middle = rest.astype(BF16).astype(F32)
    return high, middle, (rest - middle).astype(BF16).astype(F32)


def wide_dot(value, matrix, transposed):
    rows = value.shape[0]
    both = jnp.concatenate(halves(value), axis=0)
    dims = (((1,), (1 if transposed else 0,)), ((), ()))
    out = lax.dot_general(both, matrix, dims, preferred_element_type=F32)
    return out[:rows] + out[rows:]


def centred(positions, side, leaf, centre):
    point = [positions[side, a, pl.ds(leaf, 1), :] for a in range(3)]
    return [point[0] - centre] + point[1:]


def square(point):
    return point[0] * point[0] + point[1] * point[1] + point[2] * point[2]


def apply_operator(
    n,
    minor,
    probes_hbm,
    positions_hbm,
    polar_hbm,
    basis_hbm,
    leaf_transfer_hbm,
    cluster_transfer_hbm,
    upper_transfer_hbm,
    cluster_coupling_hbm,
    upper_coupling_hbm,
    near_lists_hbm,
    cluster_lists_hbm,
    upper_lists_hbm,
    out,
    probes,
    positions,
    polar,
    basis,
    leaf_transfer,
    cluster_transfer,
    upper_transfer,
    coupling,
    wide,
    coefs,
    moments,
    source_rows,
    target_rows,
    rows,
    total,
    matrices,
    level,
    near_lists,
    cluster_lists,
    upper_lists,
    load_sem,
    coupling_sem,
    coef_send,
    coef_recv,
    halo_send,
    halo_recv,
):
    leaves = probes.shape[1]
    slots = near_lists.shape[1]
    far_slots = cluster_lists.shape[1]
    vectors = wide.shape[2]
    leaf_size = wide.shape[3]
    rank = basis.shape[2]
    me = lax.axis_index("gx") * minor + lax.axis_index("gy")

    def at(device):
        return {"gx": device // minor, "gy": lax.rem(device, minor)}

    def place_of(lev):
        return n - (n >> lev - 1) + (me >> lev)

    def load(k, source, target):
        copy = pltpu.make_async_copy(source, target, load_sem.at[k])
        copy.start()
        return copy

    barrier = pltpu.get_barrier_semaphore()

    @pl.loop(1, n)
    def _(k):
        pl.semaphore_signal(
            barrier, inc=1, device_id=at(lax.rem(me + k, n)), device_id_type=MESH
        )

    first_loads = [
        load(2, positions_hbm, positions.at[1]),
        load(0, polar_hbm, polar.at[1]),
        load(1, probes_hbm, probes.at[1]),
    ]
    basis_loads = [
        load(3, basis_hbm, basis),
        load(4, leaf_transfer_hbm, leaf_transfer),
        load(5, cluster_transfer_hbm, cluster_transfer),
    ]
    list_loads = [
        load(8, near_lists_hbm, near_lists),
        load(9, cluster_lists_hbm, cluster_lists),
        load(10, upper_lists_hbm, upper_lists),
    ]
    far_loads = [
        load(6, upper_transfer_hbm, upper_transfer),
        load(7, cluster_coupling_hbm.at[0], coupling.at[0]),
    ]
    for lev in range(1, UP + 1):
        copy = pltpu.make_async_copy(
            upper_coupling_hbm.at[place_of(lev)], coupling.at[lev], coupling_sem.at[lev]
        )
        copy.start()
        far_loads.append(copy)

    def coef_copy(k, source):
        return pltpu.make_async_remote_copy(
            src_ref=coefs.at[source],
            dst_ref=coefs.at[source],
            send_sem=coef_send.at[k],
            recv_sem=coef_recv.at[source],
            device_id=at(lax.rem(me + k, n)),
            device_id_type=MESH,
        )

    def halo(side, part, device):
        source, target = (
            (positions_hbm, positions),
            (polar_hbm, polar),
            (probes_hbm, probes),
        )[part]
        return pltpu.make_async_remote_copy(
            src_ref=source,
            dst_ref=target.at[2 * side],
            send_sem=halo_send.at[side, part],
            recv_sem=halo_recv.at[side, part],
            device_id=at(device),
            device_id_type=MESH,
        )

    after = lax.rem(me + 1, n)
    before = lax.rem(me + n - 1, n)

    rows[...] = jnp.zeros(rows.shape, F32)
    source_rows[...] = jnp.zeros(source_rows.shape, BF16)
    moments[3 * leaves] = jnp.zeros(moments.shape[1:], BF16)
    pl.semaphore_wait(barrier, n - 1)

    @pl.when(me < n - 1)
    def _():
        for part in range(3):
            halo(0, part, after).start()

    @pl.when(me > 0)
    def _():
        for part in range(3):
            halo(1, part, before).start()

    for copy in first_loads:
        copy.wait()

    def scaled_probes(side, leaf):
        root = jnp.sqrt(polar[side, pl.ds(leaf, 1), :])
        return [(root * probes[side, leaf, a].astype(F32)).astype(BF16) for a in range(3)]

    for t in range(leaves):
        for a, value in enumerate(scaled_probes(1, t)):
            wide[t, a] = value

    for copy in basis_loads:
        copy.wait()
    cluster = None
    for t in range(leaves):
        coef = None
        for a in range(3):
            part = lax.dot_general(
                wide[t, a], basis[t, a], (((1,), (1,)), ((), ())), preferred_element_type=F32
            )
            coef = part if coef is None else coef + part
        carried = wide_dot(coef, leaf_transfer[t], False)
        cluster = carried if cluster is None else cluster + carried
    lifted = wide_dot(cluster, cluster_transfer[0], False)
    coefs[me] = jnp.concatenate([cluster, lifted], axis=1)

    @pl.loop(1, n)
    def _(k):
        coef_copy(k, me).start()

    centre = (2 * leaves * me + leaves - 1).astype(F32)
    first = (me - 1) * leaves
    empty = 3 * leaves

    def fill(point, factor, own):
        base = 0
        for a in range(3):
            one, two, three = thirds(point[a] * factor)
            order = (one, one, two, two, one, three) if own else (one, two, one, two, three, one)
            for k, row in enumerate(order):
                rows[base + k : base + k + 1, :] = row
            base += 6
        norm = thirds(square(point) + (1.0 if own else 0.0))
        ones = jnp.ones_like(norm[0])
        for k in range(3):
            rows[base + k : base + k + 1, :] = norm[k] if own else ones
            rows[base + 3 + k : base + 4 + k, :] = ones if own else norm[k]

    def prepare(side, leaf):
        s = side * leaves + leaf
        point = centred(positions, side, leaf, centre)
        held = scaled_probes(side, leaf) if side != 1 else [wide[leaf, a] for a in range(3)]
        x = [held[a].astype(F32) for a in range(3)]
        along = point[0] * x[0] + point[1] * x[1] + point[2] * x[2]
        norm = square(point)
        parts = [point[a] * x[b] for a in range(3) for b in range(3)]
        parts += [3.0 * point[a] * along - norm * x[a] for a in range(3)]
        for a in range(3):
            moments[s, a * vectors : (a + 1) * vectors, :] = held[a]
        for k, part in enumerate(parts):
            high, low = halves(part)
            place = (3 + k) * vectors
            moments[s, place : place + vectors, :] = high
            place = (15 + k) * vectors
            moments[s, place : place + vectors, :] = low

    def prepare_rows(side, leaf):
        fill(centred(positions, side, leaf, centre), -2.0, False)
        source_rows[side * leaves + leaf, :, :USED] = rows[:USED, :].T.astype(BF16)

    def kernel_matrix(site, target):
        radius = jnp.dot(source_rows[site], target, preferred_element_type=F32)
        inverse = lax.rsqrt(radius)
        weight = inverse * inverse
        return (weight * weight * inverse).astype(BF16)

    @pl.loop(0, leaves)
    def _(t):
        prepare(1, t)
        prepare_rows(1, t)
        fill(centred(positions, 1, t, centre), 1.0, True)
        target_rows[t] = rows[...].astype(BF16)

    @pl.loop(0, leaves)
    def _(t):
        matrix = kernel_matrix(leaves + t, target_rows[t])
        total[t] = jnp.dot(moments[leaves + t], matrix, preferred_element_type=F32)

    @pl.when(me > 0)
    def _():
        halo(0, 0, before).wait_recv()

    @pl.when(me < n - 1)
    def _():
        halo(1, 0, after).wait_recv()

    for copy in list_loads:
        copy.wait()

    @pl.loop(0, leaves)
    def _(t):
        prepare_rows(0, t)
        prepare_rows(2, t)

    def site_of(t, slot):
        source = near_lists[t, slot]
        return source, jnp.clip(source - first, 0, empty - 1)

    @pl.loop(0, leaves)
    def _(t):
        target = target_rows[t]
        for slot in range(1, slots):
            source, site = site_of(t, slot)
            block = kernel_matrix(jnp.where(source >= 0, site, leaves + t), target)
            matrices[t, (slot - 1) * leaf_size : slot * leaf_size, :] = block

    for copy in far_loads:
        copy.wait()

    @pl.loop(1, n)
    def _(k):
        coef_copy(k, lax.rem(me + k, n)).wait_recv()

    for node in range(n // 2):
        level[node] = coefs[2 * node, :, rank:] + coefs[2 * node + 1, :, rank:]
    for lev in range(1, UP):
        start = n - (n >> lev - 1)
        above = n - (n >> lev)
        for node in range(n >> lev + 1):
            place = start + 2 * node
            level[above + node] = wide_dot(
                level[place], upper_transfer[place], False
            ) + wide_dot(level[place + 1], upper_transfer[place + 1], False)
    fields = []
    for lev in range(UP + 1):
        field = None
        for s in range(far_slots):
            if lev == 0:
                source = coefs[cluster_lists[0, s], :, :rank]
            else:
                source = level[n - (n >> lev - 1) + upper_lists[s, place_of(lev)]]
            term = wide_dot(source, coupling[lev, s], True)
            field = term if field is None else field + term
        fields.append(field)
    down = fields[UP]
    for lev in range(UP - 1, -1, -1):
        matrix = upper_transfer[place_of(lev)] if lev else cluster_transfer[0]
        down = fields[lev] + wide_dot(down, matrix, True)

    @pl.when(me > 0)
    def _():
        for part in (1, 2):
            halo(0, part, before).wait_recv()

        @pl.loop(0, leaves)
        def _(t):
            prepare(0, t)

    @pl.when(me < n - 1)
    def _():
        for part in (1, 2):
            halo(1, part, after).wait_recv()

        @pl.loop(0, leaves)
        def _(t):
            prepare(2, t)

    for t in range(leaves):
        values = []
        for slot in range(1, slots):
            source, site = site_of(t, slot)
            values.append(moments[jnp.where(source >= 0, site, empty)])
        total[t] += jnp.dot(
            jnp.concatenate(values, axis=1), matrices[t], preferred_element_type=F32
        )

        point = centred(positions, 1, t, centre)
        norm = square(point) + 1.0
        root = jnp.sqrt(polar[1, pl.ds(t, 1), :])

        def group(k):
            return total[t, k * vectors : (k + 1) * vectors, :]

        def both(k):
            return group(3 + k) + group(15 + k)

        plain = [group(a) for a in range(3)]
        cross = [[both(3 * a + b) for b in range(3)] for a in range(3)]
        trace = cross[0][0] + cross[1][1] + cross[2][2]
        inner = point[0] * plain[0] + point[1] * plain[1] + point[2] * plain[2]
        leaf_field = wide_dot(down, leaf_transfer[t], True).astype(BF16)
        for a in range(3):
            value = 3.0 * point[a] * (inner - trace) + both(9 + a) - norm * plain[a]
            for b in range(3):
                value += point[b] * (2.0 * cross[b][a] - 3.0 * cross[a][b])
            far = jnp.dot(leaf_field, basis[t, a], preferred_element_type=F32)
            out[t, a] = ((value + far) * root).astype(BF16)

    @pl.loop(1, n)
    def _(k):
        coef_copy(k, me).wait_send()

    @pl.when(me < n - 1)
    def _():
        for part in range(3):
            halo(0, part, after).wait_send()

    @pl.when(me > 0)
    def _():
        for part in range(3):
            halo(1, part, before).wait_send()


def shards(
    n,
    minor,
    probes,
    positions,
    polar,
    basis,
    leaf_transfer,
    cluster_transfer,
    upper_transfer,
    cluster_coupling,
    upper_coupling,
    near_lists,
    cluster_lists,
    upper_lists,
):
    leaves, vectors, _, leaf_size = probes.shape
    probes = jnp.transpose(probes, (0, 2, 1, 3))
    basis = jnp.transpose(basis, (0, 2, 1, 3))
    positions = jnp.transpose(positions, (1, 0, 2))
    rank = leaf_transfer.shape[1]
    groups = 27 * vectors
    slots = cluster_coupling.shape[1]

    def like(array):
        return pltpu.VMEM(array.shape, array.dtype)

    applied = pl.pallas_call(
        functools.partial(apply_operator, n, minor),
        out_shape=jax.ShapeDtypeStruct((leaves, 3, vectors, leaf_size), BF16),
        in_specs=[ANY] * 12,
        out_specs=pl.BlockSpec(memory_space=pltpu.VMEM),
        scratch_shapes=[
            pltpu.VMEM((3, *probes.shape), BF16),
            pltpu.VMEM((3, *positions.shape), F32),
            pltpu.VMEM((3, *polar.shape), F32),
            like(basis),
            like(leaf_transfer),
            like(cluster_transfer),
            like(upper_transfer),
            pltpu.VMEM((UP + 1, slots, rank, rank), BF16),
            like(probes),
            pltpu.VMEM((n, vectors, 2 * rank), F32),
            pltpu.VMEM((3 * leaves + 1, groups, leaf_size), BF16),
            pltpu.VMEM((3 * leaves, leaf_size, FEATURES), BF16),
            pltpu.VMEM((leaves, FEATURES, leaf_size), BF16),
            pltpu.VMEM((FEATURES, leaf_size), F32),
            pltpu.VMEM((leaves, groups, leaf_size), F32),
            pltpu.VMEM((leaves, (near_lists.shape[1] - 1) * leaf_size, leaf_size), BF16),
            pltpu.VMEM((n, vectors, rank), F32),
            pltpu.SMEM(near_lists.shape, jnp.int32),
            pltpu.SMEM(cluster_lists.shape, jnp.int32),
            pltpu.SMEM(upper_lists.shape[::-1], jnp.int32),
            pltpu.SemaphoreType.DMA((11,)),
            pltpu.SemaphoreType.DMA((UP + 1,)),
            pltpu.SemaphoreType.DMA((n,)),
            pltpu.SemaphoreType.DMA((n,)),
            pltpu.SemaphoreType.DMA((2, 3)),
            pltpu.SemaphoreType.DMA((2, 3)),
        ],
        compiler_params=pltpu.CompilerParams(
            collective_id=0, has_side_effects=True, vmem_limit_bytes=56 << 20
        ),
        name="apply_operator",
    )(
        probes,
        positions,
        polar,
        basis,
        leaf_transfer,
        cluster_transfer,
        upper_transfer,
        cluster_coupling,
        upper_coupling,
        near_lists,
        cluster_lists,
        upper_lists.T,
    )
    return jnp.transpose(applied, (0, 2, 1, 3))


def solution(mesh):
    n = mesh.shape["gx"] * mesh.shape["gy"]
    split = ("groups", "gx", "gy")
    in_specs = (
        P(split, None, None, None),
        P(split, None, None),
        P(split, None),
        P(split, None, None, None),
        P(split, None, None),
        P(split, None, None),
        P("groups", None, None),
        P(split, None, None, None),
        P("groups", None, None, None),
        P(split, None),
        P(split, None),
        P("groups", None),
    )
    return jax.shard_map(
        functools.partial(shards, n, mesh.shape["gy"]),
        mesh=mesh,
        in_specs=in_specs,
        out_specs=P(split, None, None, None),
        check_vma=False,
    )
```
